768 devices in a mesh: rows: 384 (over x, y, z), grp: 2 (over core).
Axes of the slice: x: 4, y: 8, z: 12, core: 2. Of those that a mesh axis runs over, the one named last changes fastest.
Arguments:
- a_tiles: bfloat16 [6144, 15, 128, 128], P(('rows', 'grp')), may hold values from -1 to 1
- a_cols: int32 [6144, 15], P(('rows', 'grp')), may hold values from 0 to 15
- a_count: int32 [768, 8], P(('rows', 'grp')), may hold values from 1 to 15, 40 in all within a row
- send_lists: int32 [768, 8], P(('rows', 'grp')), may hold values from 0 to 7
- ghost_cols: int32 [768, 8], P(('rows', 'grp')), may hold values from 0 to 5
- cmap: int32 [6144], P(('rows', 'grp')), may hold values from 0 to 1
- p_tiles: bfloat16 [6144, 128, 128], P(('rows', 'grp')), may hold values from -0.5 to 0.5
- x_start: float32 [768, 128], P(('rows', 'grp')), may hold values from -6 to 6
- coarse_rhs: float32 [768, 128], P(('rows', 'grp')), may hold values from -24 to 24
Outputs:
- coarse_op: float32 [768, 128, 768], P(('rows', 'grp'))
- coarse_sol: float32 [768, 128], P(('rows', 'grp'))
The draws below stay inside these ranges and needn't reach their ends.
Inputs may be any that keep to these rules, and one draw needn't show every extreme that they name: `a_count`: each device's 8 counts sum to 40 and the largest of them is exactly 15. `a_cols`: slots at or beyond a row's count carry no entry; values 0 to 7 are own blocks, 8 to 11 the lower ghosts, the rest the upper ghosts.
All inputs are finite; a program needn't handle non-finite values.
Results may differ from the reference program's by a relative error of at most 0.003.
Values may be sent and summed in bfloat16 or wider, within the bound.
No kernel may reach another device: no remote copies, remote signals or barrier semaphores. Data moves between devices by JAX's collectives and lax.ppermute only.
A program may use at most 64 MiB of HBM per device.

```python
import math
import jax
import jax.numpy as jnp
import numpy as np
from jax import lax

B = 128
RB = 8
K = 15
G = 4
CC = 2
NB = 6144
NC = 768
N_ROWS = 384
N_GRP = 2


def plant(result, stream_key, least, high):
    extent = result.shape
    spot = [jax.random.randint(jax.random.fold_in(stream_key, axis), (), 0, extent[axis]) for axis in range(len(extent))]
    result = result.at[tuple(spot)].set(least)
    longest = extent.index(max(extent))
    spot[longest] = (spot[longest] + 1) % extent[longest]
    return result.at[tuple(spot)].set(high)


def steps_of(stream_key, extent, shards, smallest, top_value):
    loudness = 1.0
    for axis_at, parts in shards:
        draws = jax.random.uniform(jax.random.fold_in(jax.random.fold_in(stream_key, 6), axis_at), (parts,), jnp.float32, smallest / len(shards), top_value / len(shards))
        loudness = loudness * jnp.repeat(jnp.exp(draws), extent[axis_at] // parts).reshape((-1,) + (1,) * (len(extent) - 1 - axis_at))
    return loudness


def split_up(number_of, total, limit, skew):
    portions = [(1 << 20) // math.isqrt(grade ** skew) + 1 for grade in range(2, number_of + 1)]
    surplus, counts = total - limit - (number_of - 1), [1] * (number_of - 1)
    while surplus > 0:
        free = [i for i in range(number_of - 1) if counts[i] < limit]
        mass, left = sum([portions[i] for i in free]), surplus
        for i in free:
            more = min(limit - counts[i], max(1, left * portions[i] // mass), surplus)
            counts[i] = counts[i] + more
            surplus = surplus - more
    return np.array([limit] + counts)


def ragged(own_key, number_of, total, most, lean):
    if number_of == 2:
        one = jax.random.randint(own_key, (), max(1, total - most), min(most, total - 1) + 1)
        return jnp.stack([one, total - one])
    sizes = jnp.asarray(split_up(number_of, total, most, lean), jnp.int32)
    twos = (number_of - 1) // 2
    giver, sink = sizes[1:1 + 2 * twos:2], sizes[2:2 + 2 * twos:2]
    slack = jnp.minimum(giver - 1, most - sink)
    passed = jax.random.randint(jax.random.fold_in(own_key, 1), (twos,), 0, 1 << 20) % (slack + 1)
    sizes = sizes.at[1:1 + 2 * twos:2].set(giver - passed).at[2:2 + 2 * twos:2].set(sink + passed)
    return sizes[jax.random.permutation(jax.random.fold_in(own_key, 2), number_of)]


def normal_values(key, extent, scale, limit, shards=(), kind=jnp.bfloat16):
    level = steps_of(key, extent, shards, -0.22, 0.18) if shards else 1.0
    drawn = jax.random.normal(key, extent, jnp.float32) * scale * level
    return jnp.minimum(jnp.maximum(drawn, -limit), limit).astype(kind)


def setup_inputs(seed: int = 0) -> dict:
    arg_keys = jax.random.split(jax.random.key(seed), 10)
    return {
        "a_tiles": normal_values(arg_keys[0], (NB, K, B, B), 0.15, 1.0, ((0, 768),)),
        "a_cols": plant(jax.random.randint(arg_keys[1], (NB, K), 0, RB + 2 * G), jax.random.fold_in(arg_keys[1], 1), 0, (RB + 2 * G) - 1).astype(jnp.int32),
        "a_count": jax.vmap(lambda own: ragged(own, RB, RB * K // 3, K, 2))(jax.random.split(arg_keys[2], (N_ROWS * N_GRP))).reshape((N_ROWS * N_GRP, RB)).astype(jnp.int32),
        "send_lists": plant(jax.random.randint(arg_keys[3], (N_ROWS * N_GRP, 2 * G), 0, RB), jax.random.fold_in(arg_keys[3], 1), 0, RB - 1).astype(jnp.int32),
        "ghost_cols": plant(jax.random.randint(arg_keys[4], (N_ROWS * N_GRP, 2 * G), 0, 3 * CC), jax.random.fold_in(arg_keys[4], 1), 0, (3 * CC) - 1).astype(jnp.int32),
        "cmap": plant(jax.random.randint(arg_keys[5], (NB,), 0, CC), jax.random.fold_in(arg_keys[5], 1), 0, CC - 1).astype(jnp.int32),
        "p_tiles": normal_values(arg_keys[6], (NB, B, B), B ** -0.5, 0.5, ((0, 768),)),
        "x_start": normal_values(arg_keys[7], (NC, B), 1.0, 6.0, ((0, 768),), jnp.float32),
        "coarse_rhs": normal_values(arg_keys[8], (NC, B), 4.0, 24.0, ((0, 768),), jnp.float32),
    }


def device_partial(a_t, a_c, count, g_cols, c_map, p_own, p_left, p_right):
    p_ext = jnp.concatenate([p_own, p_left, p_right], axis=0)
    picked = jnp.take(p_ext, a_c, axis=0)
    prod = jnp.einsum("ismn,isnl->isml", a_t.astype(jnp.float32), picked.astype(jnp.float32)).astype(jnp.bfloat16)
    tiles = jnp.einsum("imk,isml->iskl", p_own.astype(jnp.float32), prod.astype(jnp.float32))
    live = (jnp.arange(K, dtype=jnp.int32)[None, :] < count[:, None]).astype(jnp.float32)
    col_map = jnp.concatenate([CC + c_map, g_cols]).astype(jnp.int32)
    col_block = jnp.take(col_map, a_c, axis=0)
    row_hot = (c_map[:, None] == jnp.arange(CC, dtype=jnp.int32)[None, :]).astype(jnp.float32)
    col_hot = (col_block[:, :, None] == jnp.arange(3 * CC, dtype=jnp.int32)[None, None, :]).astype(jnp.float32) * live[:, :, None]
    weights = row_hot[:, None, :, None] * col_hot[:, :, None, :]
    partial_value = jnp.einsum("isIJ,iskl->IkJl", weights, tiles, precision=lax.Precision.HIGHEST)
    return partial_value.reshape(CC, B, 3 * CC * B)


def reference(a_tiles, a_cols, a_count, send_lists, ghost_cols, cmap, p_tiles, x_start, coarse_rhs):
    devs = N_ROWS * N_GRP
    p_dev = p_tiles.reshape(devs, RB, B, B)
    send_all = jax.vmap(lambda p, s: jnp.take(p, s, axis=0))(p_dev, send_lists)
    empty = jnp.zeros((1, G, B, B), jnp.bfloat16)
    left_all = jnp.concatenate([empty, send_all[:-1, G:]], axis=0)
    right_all = jnp.concatenate([send_all[1:, :G], empty], axis=0)
    chip_args = (a_tiles.reshape(N_ROWS, 2, RB, K, B, B), a_cols.reshape(N_ROWS, 2, RB, K),
                 a_count.reshape(N_ROWS, 2, RB), ghost_cols.reshape(N_ROWS, 2, 2 * G),
                 cmap.reshape(N_ROWS, 2, RB), p_dev.reshape(N_ROWS, 2, RB, B, B),
                 left_all.reshape(N_ROWS, 2, G, B, B), right_all.reshape(N_ROWS, 2, G, B, B))

    def chip_sum(args):
        first = device_partial(*[a[0] for a in args])
        second = device_partial(*[a[1] for a in args])
        return first + second

    coarse_op = lax.map(chip_sum, chip_args).reshape(NC, B, 3 * CC * B)
    chip_mats = coarse_op.reshape(N_ROWS, CC * B, 3 * CC * B)

    def apply(vec):
        rows_vec = vec.reshape(N_ROWS, CC * B)
        zero_row = jnp.zeros((1, CC * B), jnp.float32)
        lower = jnp.concatenate([zero_row, rows_vec[:-1]], axis=0)
        upper = jnp.concatenate([rows_vec[1:], zero_row], axis=0)
        ext = jnp.concatenate([lower, rows_vec, upper], axis=1)
        return jnp.einsum("cij,cj->ci", chip_mats, ext, precision=lax.Precision.HIGHEST).reshape(NC, B)

    theta = 13.0
    delta = 11.0
    sigma = theta / delta
    rho_zero = 1.0 / sigma
    resid = coarse_rhs - apply(x_start)
    step_zero = resid / theta
    first_x = x_start + step_zero
    resid = resid - apply(step_zero)
    rho_one = 1.0 / (2.0 * sigma - rho_zero)
    step_one = rho_one * rho_zero * step_zero + (2.0 * rho_one / delta) * resid
    return coarse_op, first_x + step_one
```

```python
import jax
import jax.numpy as jnp
from jax import lax
from jax.experimental import pallas as pl
from jax.experimental.pallas import tpu as pltpu
from jax.sharding import PartitionSpec as P

B = 128
RB = 8
K = 15
G = 4
CC = 2
NJ = 3 * CC
NLIVE = 40
VECS = 16
MSG = 8 * B + 8

THETA = 13.0
DELTA = 11.0
SIGMA = THETA / DELTA
RHO0 = 1.0 / SIGMA
RHO1 = 1.0 / (2.0 * SIGMA - RHO0)

F32 = jnp.float32
BF16 = jnp.bfloat16
AXES = ("rows", "grp")
HBM = pl.BlockSpec(memory_space=pltpu.HBM)
VMEM = pl.BlockSpec(memory_space=pltpu.VMEM)
DMA = pltpu.SemaphoreType.DMA


def split3(x):
    hi = x.astype(BF16).astype(F32)
    mid = (x - hi).astype(BF16).astype(F32)
    return [hi, mid, x - hi - mid]


def padded(parts):
    rows = sum(part.shape[0] for part in parts)
    return jnp.concatenate(parts + [jnp.zeros((VECS - rows, B), F32)], axis=0).astype(BF16)


def matvec(blocks, vecs):
    acc = blocks[0] * vecs[0]
    for blk, vec in zip(blocks[1:], vecs[1:]):
        acc = acc + blk * vec
    return jnp.sum(acc.T, axis=0, keepdims=True)


def pack_kernel(send, p, x, out_a, out_b, p_out, send_s, x_v, sems):
    g = lax.axis_index("grp")
    copies = [
        pltpu.make_async_copy(send, send_s, sems.at[0]),
        pltpu.make_async_copy(p, p_out, sems.at[1]),
        pltpu.make_async_copy(x, x_v, sems.at[2]),
    ]
    for copy in copies:
        copy.start()
    for copy in copies:
        copy.wait()
    for k in range(G):
        out_a[k * B : (k + 1) * B, :] = p_out[send_s[0, G * (1 - g) + k]]
        out_b[k * B : (k + 1) * B, :] = p_out[send_s[0, G * g + k]]
    out_a[G * B :, :] = padded(split3(x_v[...]))


def pair_kernel(got_a, b_in, out_b, x_out):
    rows = [got_a[c, G * B :, :].astype(F32) for c in range(CC)]
    terms = [jnp.concatenate([r[k : k + 1] for r in rows], axis=0) for k in range(3)]
    out_b[: G * B, :] = b_in[: G * B, :]
    out_b[G * B :, :] = padded(terms)
    x_out[...] = terms[0] + terms[1] + terms[2]


def coarse_kernel(cols, count, ghost, cmap, a, p, got_a, mh, mg, tb, t, pt, cols_s, count_s, ghost_s, cmap_s, sems):
    g = lax.axis_index("grp")
    h = 1 - g
    copies = [
        pltpu.make_async_copy(src, dst, sems.at[n])
        for n, (src, dst) in enumerate([(cols, cols_s), (count, count_s), (ghost, ghost_s), (cmap, cmap_s)])
    ]
    for copy in copies:
        copy.start()
    t[...] = jnp.zeros_like(t)
    mh[...] = jnp.zeros_like(mh)
    mg[...] = jnp.zeros_like(mg)
    for i in range(RB):
        pt[i] = p[i].T
    for copy in copies:
        copy.wait()
    i = jnp.int32(0)
    s = jnp.int32(0)
    for n in range(NLIVE):
        r = jnp.where(cmap_s[i] == g, 1, 0)
        t[cols_s[i, s], r] += jnp.dot(pt[i], a[i, s], preferred_element_type=F32)
        if n + 1 < NLIVE:
            over = s + 1 >= count_s[0, i]
            s = jnp.where(over, 0, s + 1)
            i = jnp.where(over, i + 1, i)

    def halves(c):
        tc = t[c].reshape(CC * B, B)
        hi = tc.astype(BF16)
        lo = (tc - hi.astype(F32)).astype(BF16)
        return jnp.concatenate([hi, lo], axis=1)

    def add(j, lhs, tile):
        out = jnp.dot(lhs, jnp.concatenate([tile, tile], axis=0), preferred_element_type=F32)
        mh[pl.ds(pl.multiple_of(j * B, B), B), :] += out[:B]
        mg[j] += out[B:]

    for c in range(RB):
        add(CC + cmap_s[c], halves(c), p[c])
    for k in range(G):
        q = G * h + k
        add(ghost_s[0, q], halves(RB + q), got_a[h, k * B : (k + 1) * B, :])
    for k in range(G):
        tb[k] = halves(RB + G * g + k)


def message_kernel(ghost, mh_in, mg_in, tb, recv, x, rhs, mh, mg, vec, ghost_s, sems):
    g = lax.axis_index("grp")
    h = 1 - g
    copy = pltpu.make_async_copy(ghost, ghost_s, sems.at[0])
    copy.start()
    mh[: NJ * B, :] = mh_in[...]
    mg[...] = mg_in[...]
    rows = recv[G * B :, :].astype(F32)
    side = rows[0:2] + rows[2:4] + rows[4:6]
    outs = []
    for k in range(G):
        tile = recv[k * B : (k + 1) * B, :]
        outs.append(jnp.dot(tb[k], jnp.concatenate([tile, tile], axis=0), preferred_element_type=F32))
    copy.wait()
    for k in range(G):
        j = ghost_s[0, G * g + k]
        mh[pl.ds(pl.multiple_of(j * B, B), B), :] += outs[k][:B]
        mg[j] += outs[k][B:]
    xs = [x[0:1, :], x[1:2, :], side[0:1], side[1:2]]
    js = [2, 3, 4 * g, 4 * g + 1]
    known_h = matvec([mh[pl.ds(pl.multiple_of(j * B, B), B), :] for j in js], xs)
    known_g = matvec([mg[j] for j in js], xs)
    for q in range(CC):
        mh[(NJ + q) * B : (NJ + q + 1) * B, :] = mg[4 * h + q]
    mh[8 * B :, :] = jnp.concatenate([rhs[...] - known_g, side, jnp.zeros((5, B), F32)], axis=0)
    vec[...] = jnp.concatenate([known_h, side, jnp.zeros((5, B), F32)], axis=0)


def step_kernel(mh, mg, msg, vec, x, rhs, mats, step, base):
    g = lax.axis_index("grp")
    h = 1 - g
    first = g == 0
    far = [msg[8 * B + 1 : 8 * B + 2, :], msg[8 * B + 2 : 8 * B + 3, :]]
    near = [vec[1:2, :], vec[2:3, :]]
    low = [jnp.where(first, n, f) for n, f in zip(near, far)]
    high = [jnp.where(first, f, n) for n, f in zip(near, far)]
    xs = low + [x[0:1, :], x[1:2, :]] + high
    blocks = []
    for j in range(NJ):
        blk = mg[j] + msg[j * B : (j + 1) * B, :]
        mats[j] = blk
        blocks.append(blk)
    resid = rhs[...] - matvec(blocks, xs)
    other = [mh[pl.ds(pl.multiple_of((4 * h + q) * B, B), B), :] for q in range(CC)]
    other += [msg[6 * B : 7 * B, :], msg[7 * B : 8 * B, :]]
    resid_h = msg[8 * B : 8 * B + 1, :] - vec[0:1, :] - matvec(other, far + near)
    d_g = resid / THETA
    d_h = resid_h / THETA
    d0 = jnp.where(first, d_g, d_h)
    d1 = jnp.where(first, d_h, d_g)
    step[...] = jnp.concatenate([d0, d1], axis=0)
    resid = resid - matvec(blocks[2:4], [d0, d1])
    x_own = jnp.where(first, x[0:1, :], x[1:2, :])
    base[...] = x_own + d_g + RHO1 * RHO0 * d_g + (2.0 * RHO1 / DELTA) * resid


def out_kernel(mats, op, sems):
    copies = [
        pltpu.make_async_copy(mats.at[j], op.at[0, :, pl.ds(j * B, B)], sems.at[j]) for j in range(NJ)
    ]
    for copy in copies:
        copy.start()
    for copy in copies:
        copy.wait()


def last_kernel(mats, ext, base, sol):
    blocks = [mats[j] for j in (0, 1, 4, 5)]
    sol[...] = base[...] - (2.0 * RHO1 / DELTA) * matvec(blocks, [ext[i : i + 1, :] for i in range(4)])


def call(kernel, out_shape, in_specs, scratch=(), out_specs=None, us=1, **kw):
    return pl.pallas_call(
        kernel,
        out_shape=out_shape,
        in_specs=in_specs,
        out_specs=out_specs or [VMEM] * len(out_shape),
        scratch_shapes=list(scratch),
        compiler_params=pltpu.CompilerParams(vmem_limit_bytes=16 << 20),
        cost_estimate=pl.CostEstimate(flops=us * 10**9, bytes_accessed=0, transcendentals=0),
        **kw,
    )


def shaped(*shape, dtype=F32):
    return jax.ShapeDtypeStruct(shape, dtype)


def ints(*shape):
    return pltpu.SMEM(shape, jnp.int32)


def on_device(a_tiles, a_cols, a_count, send_lists, ghost_cols, cmap, p_tiles, x_start, coarse_rhs):
    rows = lax.axis_size("rows")
    across, swap = [], []
    for c in range(rows):
        swap += [(2 * c, 2 * c + 1), (2 * c + 1, 2 * c)]
        if c + 1 < rows:
            across += [(2 * c + 1, 2 * c + 2), (2 * c + 2, 2 * c + 1)]

    send_a, send_b, p = call(
        pack_kernel,
        [shaped(G * B + VECS, B, dtype=BF16), shaped(G * B + VECS, B, dtype=BF16), shaped(RB, B, B, dtype=BF16)],
        [HBM] * 3,
        [ints(1, 8), pltpu.VMEM((1, B), F32), DMA((3,))],
    )(send_lists, p_tiles, x_start)
    got_a = lax.all_gather(send_a, "grp", axis=0)
    send_b, x = call(
        pair_kernel,
        [shaped(G * B + VECS, B, dtype=BF16), shaped(CC, B)],
        [VMEM] * 2,
    )(got_a, send_b)
    recv_b = lax.ppermute(send_b, AXES, across)
    mh, mg, tb = call(
        coarse_kernel,
        [shaped(NJ * B, B), shaped(NJ, B, B), shaped(G, CC * B, 2 * B, dtype=BF16)],
        [HBM] * 4 + [VMEM] * 3,
        [
            pltpu.VMEM((RB + 2 * G, CC, B, B), F32),
            pltpu.VMEM((RB, B, B), BF16),
            ints(8, 15),
            ints(1, 8),
            ints(1, 8),
            ints(8),
            DMA((4,)),
        ],
    )(a_cols, a_count, ghost_cols, cmap, a_tiles, p, got_a)
    mh, mg, vec = call(
        message_kernel,
        [shaped(MSG, B), shaped(NJ, B, B), shaped(8, B)],
        [HBM] + [VMEM] * 6,
        [ints(1, 8), DMA((1,))],
    )(ghost_cols, mh, mg, tb, recv_b, x, coarse_rhs)
    msg = lax.ppermute(mh, AXES, swap)
    mats, step, base = call(
        step_kernel,
        [shaped(NJ, B, B), shaped(CC, B), shaped(1, B)],
        [VMEM] * 6,
    )(mh, mg, msg, vec, x, coarse_rhs)
    beyond = lax.ppermute(step, AXES, across)
    (op,) = call(
        out_kernel, [shaped(1, B, NJ * B)], [VMEM], [DMA((NJ,))], out_specs=[HBM]
    )(mats)
    ext = lax.all_gather(beyond, "grp", axis=0, tiled=True)
    (sol,) = call(last_kernel, [shaped(1, B)], [VMEM] * 3)(mats, ext, base)
    return op, sol


def solution(mesh):
    two = P(AXES, None)
    three = P(AXES, None, None)
    return jax.shard_map(
        on_device,
        mesh=mesh,
        in_specs=(P(AXES, None, None, None), two, two, two, two, P(AXES), three, two, two),
        out_specs=(three, two),
        check_vma=False,
    )
```

```python
import jax
import jax.numpy as jnp
from jax import lax
from jax.experimental import pallas as pl
from jax.experimental.pallas import tpu as pltpu
from jax.sharding import PartitionSpec as P

B = 128
RB = 8
K = 15
G = 4
CC = 2
NJ = 3 * CC
NLIVE = 40
VECS = 16
COARSE_US = 0
FIRST_US = 5
AFTER_US = 5

THETA = 13.0
DELTA = 11.0
SIGMA = THETA / DELTA
RHO0 = 1.0 / SIGMA
RHO1 = 1.0 / (2.0 * SIGMA - RHO0)

F32 = jnp.float32
BF16 = jnp.bfloat16
AXES = ("rows", "grp")
HBM = pl.BlockSpec(memory_space=pltpu.HBM)
ANY = pl.BlockSpec(memory_space=pl.ANY)
VMEM = pl.BlockSpec(memory_space=pltpu.VMEM)
DMA = pltpu.SemaphoreType.DMA


def split3(x):
    hi = x.astype(BF16).astype(F32)
    mid = (x - hi).astype(BF16).astype(F32)
    return [hi, mid, x - hi - mid]


def padded(parts):
    rows = sum(part.shape[0] for part in parts)
    return jnp.concatenate(parts + [jnp.zeros((VECS - rows, B), F32)], axis=0).astype(BF16)


def matvec(blocks, vecs):
    acc = blocks[0] * vecs[0]
    for blk, vec in zip(blocks[1:], vecs[1:]):
        acc = acc + blk * vec
    return jnp.sum(acc.T, axis=0, keepdims=True)


def first_kernel(out):
    out[...] = jnp.zeros_like(out)


def pack_kernel(zero, send, p, x, out_a, out_b, out_p):
    first = lax.axis_index("grp") == 0
    lists = send[...]
    low = [lists[0, k] for k in range(G)]
    high = [lists[0, G + k] for k in range(G)]
    out_a[G * B :, :] = padded(split3(x[...] + zero[0:1, :]))
    out_p[...] = p[...]
    for k in range(G):
        out_a[k * B : (k + 1) * B, :] = p[jnp.where(first, high[k], low[k])]
        out_b[k * B : (k + 1) * B, :] = p[jnp.where(first, low[k], high[k])]


def pair_kernel(got_a, tiles, out_b, x):
    rows = [got_a[c, G * B :, :].astype(F32) for c in range(CC)]
    terms = [jnp.concatenate([r[k : k + 1] for r in rows], axis=0) for k in range(3)]
    out_b[: G * B, :] = tiles[...]
    out_b[G * B :, :] = padded(terms)
    x[...] = terms[0] + terms[1] + terms[2]


def coarse_kernel(cols, count, ghost, cmap, a, p, got_a, mh, mg, tb, t, pt, cols_s, count_s, ghost_s, cmap_s, sems):
    g = lax.axis_index("grp")
    h = 1 - g
    copies = [
        pltpu.make_async_copy(src, dst, sems.at[n])
        for n, (src, dst) in enumerate([(cols, cols_s), (count, count_s), (ghost, ghost_s), (cmap, cmap_s)])
    ]
    for copy in copies:
        copy.start()
    t[...] = jnp.zeros_like(t)
    mh[...] = jnp.zeros_like(mh)
    mg[...] = jnp.zeros_like(mg)
    for i in range(RB):
        pt[i] = p[i].T
    for copy in copies:
        copy.wait()
    i = jnp.int32(0)
    s = jnp.int32(0)
    for n in range(NLIVE):
        r = jnp.where(cmap_s[i] == g, 1, 0)
        t[cols_s[i, s], r] += jnp.dot(pt[i], a[i, s], preferred_element_type=F32)
        if n + 1 < NLIVE:
            over = s + 1 >= count_s[0, i]
            s = jnp.where(over, 0, s + 1)
            i = jnp.where(over, i + 1, i)

    def halves(c):
        tc = t[c].reshape(CC * B, B)
        hi = tc.astype(BF16)
        lo = (tc - hi.astype(F32)).astype(BF16)
        return jnp.concatenate([hi, lo], axis=1)

    def add(j, lhs, tile):
        out = jnp.dot(lhs, jnp.concatenate([tile, tile], axis=0), preferred_element_type=F32)
        mh[j] += out[:B]
        mg[j] += out[B:]

    for c in range(RB):
        add(CC + cmap_s[c], halves(c), p[c])
    for k in range(G):
        q = G * h + k
        add(ghost_s[0, q], halves(RB + q), got_a[h, k * B : (k + 1) * B, :])
    for k in range(G):
        tb[k] = halves(RB + G * g + k)


def known(g):
    return [4 * g, 4 * g + 1]


def message_kernel(ghost, recv, mh_in, mg_in, tb, x, rhs, mh, mg, ext, vec):
    g = lax.axis_index("grp")
    first = g == 0
    lists = ghost[...]
    js = [jnp.where(first, lists[0, k], lists[0, G + k]) for k in range(G)]
    mh[...] = mh_in[...]
    mg[...] = mg_in[...]
    outs = []
    for k in range(G):
        tile = recv[k * B : (k + 1) * B, :]
        outs.append(jnp.dot(tb[k], jnp.concatenate([tile, tile], axis=0), preferred_element_type=F32))
    for k in range(G):
        j = js[k]
        mh[j] += outs[k][:B]
        mg[j] += outs[k][B:]
    rows = recv[G * B :, :].astype(F32)
    near = rows[0:2] + rows[2:4] + rows[4:6]
    xs = [x[0:1, :], x[1:2, :], near[0:1], near[1:2]]
    js = [2, 3] + known(g)
    w_h = matvec([mh[j] for j in js], xs)
    w_g = matvec([mg[j] for j in js], xs)
    for j in range(NJ):
        hi = mh[j].astype(BF16)
        ext[j * B : (j + 1) * B, :] = hi
        ext[(NJ + j) * B : (NJ + j + 1) * B, :] = (mh[j] - hi.astype(F32)).astype(BF16)
    for q, j in enumerate(known(1 - g)):
        ext[(2 * NJ + q) * B : (2 * NJ + q + 1) * B, :] = mg[j].astype(BF16)
    rows = jnp.concatenate([w_h, rhs[...] - w_g, near], axis=0)
    ext[14 * B :, :] = padded(split3(rows))
    vec[...] = rows


def wide(exts, c, j):
    return (
        exts[c, pl.ds(pl.multiple_of(j * B, B), B), :].astype(F32)
        + exts[c, pl.ds(pl.multiple_of((NJ + j) * B, B), B), :].astype(F32)
    )


def step_kernel(exts, mh, mg, vec, x, step, base):
    g = lax.axis_index("grp")
    h = 1 - g
    first = g == 0
    rows = exts[h, 14 * B :, :].astype(F32)
    far = rows[0:4] + rows[4:8] + rows[8:12]
    xs = [far[2:3], far[3:4], vec[2:3, :], vec[3:4, :]]
    in_g = [mg[j] for j in known(h)] + [wide(exts, h, j) for j in known(g)]
    in_h = [mh[j] for j in known(h)] + [exts[h, (12 + q) * B : (13 + q) * B, :].astype(F32) for q in range(CC)]
    resid = vec[1:2, :] - far[0:1] - matvec(in_g, xs)
    resid_h = far[1:2] - vec[0:1, :] - matvec(in_h, xs)
    d_g = resid / THETA
    d_h = resid_h / THETA
    step[...] = jnp.concatenate([jnp.where(first, d_g, d_h), jnp.where(first, d_h, d_g)], axis=0)
    x_own = jnp.where(first, x[0:1, :], x[1:2, :])
    base[...] = x_own + d_g + RHO1 * RHO0 * d_g + (2.0 * RHO1 / DELTA) * resid


def sum_kernel(mg, exts, step, base_in, mats, base, op, sems):
    h = 1 - lax.axis_index("grp")
    copies = []
    for j in range(NJ):
        mats[j] = mg[j] + wide(exts, h, j)
        copies.append(pltpu.make_async_copy(mats.at[j], op.at[0, :, pl.ds(j * B, B)], sems.at[j]))
        copies[-1].start()
    own = matvec([mats[2], mats[3]], [step[0:1, :], step[1:2, :]])
    base[...] = base_in[...] - (2.0 * RHO1 / DELTA) * own
    for copy in copies:
        copy.wait()


def last_kernel(mats, ext, base, sol):
    blocks = [mats[j] for j in (0, 1, 4, 5)]
    sol[...] = base[...] - (2.0 * RHO1 / DELTA) * matvec(blocks, [ext[i : i + 1, :] for i in range(4)])


def call(kernel, out_shape, in_specs, scratch=(), out_specs=None, us=1, vm=16, **kw):
    return pl.pallas_call(
        kernel,
        out_shape=out_shape,
        in_specs=in_specs,
        out_specs=out_specs or [VMEM] * len(out_shape),
        scratch_shapes=list(scratch),
        compiler_params=pltpu.CompilerParams(vmem_limit_bytes=vm << 20),
        cost_estimate=pl.CostEstimate(flops=us * 10**9, bytes_accessed=0, transcendentals=0),
        **kw,
    )


def after_kernel(*refs):
    pass


def after(value, *others):
    (out,) = call(
        after_kernel,
        [shaped(*value.shape, dtype=value.dtype)],
        [ANY] * (1 + len(others)),
        out_specs=[ANY],
        input_output_aliases={0: 0},
        us=AFTER_US,
    )(value, *others)
    return out


def shaped(*shape, dtype=F32):
    return jax.ShapeDtypeStruct(shape, dtype)


def ints(*shape):
    return pltpu.SMEM(shape, jnp.int32)


def on_device(a_tiles, a_cols, a_count, send_lists, ghost_cols, cmap, p_tiles, x_start, coarse_rhs):
    rows = lax.axis_size("rows")
    near = []
    for c in range(rows - 1):
        near += [(2 * c + 1, 2 * c + 2), (2 * c + 2, 2 * c + 1)]

    part = shaped(NJ, B, B)
    packed = shaped(G * B + VECS, B, dtype=BF16)
    (zero,) = call(first_kernel, [shaped(8, B)], [], us=FIRST_US)()
    send_a, send_b, p = call(
        pack_kernel,
        [packed, shaped(G * B, B, dtype=BF16), shaped(RB, B, B, dtype=BF16)],
        [VMEM] * 4,
    )(zero, send_lists, p_tiles, x_start)
    got_a = lax.all_gather(send_a, "grp", axis=0)
    send_b, x = call(pair_kernel, [packed, shaped(CC, B)], [VMEM] * 2)(got_a, send_b)
    recv_b = lax.ppermute(send_b, AXES, near)
    mh, mg, tb = call(
        coarse_kernel,
        [part, part, shaped(G, CC * B, 2 * B, dtype=BF16)],
        [HBM] * 4 + [VMEM] * 3,
        [
            pltpu.VMEM((RB + 2 * G, CC, B, B), F32),
            pltpu.VMEM((RB, B, B), BF16),
            ints(8, 15),
            ints(1, 8),
            ints(1, 8),
            ints(8),
            DMA((4,)),
        ],
        us=COARSE_US,
    )(a_cols, a_count, ghost_cols, cmap, a_tiles, p, got_a)
    mh, mg, ext, vec = call(
        message_kernel,
        [part, part, shaped(14 * B + VECS, B, dtype=BF16), shaped(4, B)],
        [VMEM] * 7,
    )(ghost_cols, recv_b, mh, mg, tb, x, coarse_rhs)
    exts = lax.all_gather(ext, "grp", axis=0)
    step, base = call(step_kernel, [shaped(CC, B), shaped(1, B)], [VMEM] * 5)(exts, mh, mg, vec, x)
    beyond = lax.ppermute(step, AXES, near)
    mats, base, op = call(
        sum_kernel,
        [part, shaped(1, B), shaped(1, B, NJ * B)],
        [VMEM] * 4,
        [DMA((NJ,))],
        out_specs=[VMEM, VMEM, HBM],
    )(mg, exts, step, base)
    around = lax.all_gather(after(beyond, base), "grp", axis=0, tiled=True)
    (sol,) = call(last_kernel, [shaped(1, B)], [VMEM] * 3)(mats, around, base)
    return op, sol


def solution(mesh):
    two = P(AXES, None)
    three = P(AXES, None, None)
    return jax.shard_map(
        on_device,
        mesh=mesh,
        in_specs=(P(AXES, None, None, None), two, two, two, two, P(AXES), three, two, two),
        out_specs=(three, two),
        check_vma=False,
    )
```

```python
import jax
import jax.numpy as jnp
from jax import lax
from jax.experimental import pallas as pl
from jax.experimental.pallas import tpu as pltpu
from jax.sharding import PartitionSpec as P

B = 128
RB = 8
K = 15
G = 4
CC = 2
NJ = 3 * CC
NLIVE = 40
VECS = 16
COARSE_US = 0
LINE = 12
FIRST_US = 1
SECOND_US = 1
AFTER_US = 5

THETA = 13.0
DELTA = 11.0
SIGMA = THETA / DELTA
RHO0 = 1.0 / SIGMA
RHO1 = 1.0 / (2.0 * SIGMA - RHO0)

F32 = jnp.float32
BF16 = jnp.bfloat16
AXES = ("rows", "grp")
HBM = pl.BlockSpec(memory_space=pltpu.HBM)
ANY = pl.BlockSpec(memory_space=pl.ANY)
VMEM = pl.BlockSpec(memory_space=pltpu.VMEM)
DMA = pltpu.SemaphoreType.DMA


def split3(x):
    hi = x.astype(BF16).astype(F32)
    mid = (x - hi).astype(BF16).astype(F32)
    return [hi, mid, x - hi - mid]


def padded(parts):
    rows = sum(part.shape[0] for part in parts)
    return jnp.concatenate(parts + [jnp.zeros((VECS - rows, B), F32)], axis=0).astype(BF16)


def matvec(blocks, vecs):
    acc = blocks[0] * vecs[0]
    for blk, vec in zip(blocks[1:], vecs[1:]):
        acc = acc + blk * vec
    return jnp.sum(acc.T, axis=0, keepdims=True)


def first_kernel(out):
    out[...] = jnp.zeros_like(out)


def pack_kernel(zero, send, p, x, out_a, out_b, out_p):
    first = lax.axis_index("grp") == 0
    lists = send[...]
    low = [lists[0, k] for k in range(G)]
    high = [lists[0, G + k] for k in range(G)]
    out_b[G * B :, :] = padded(split3(x[...] + zero[0:1, :]))
    out_p[...] = p[...]
    for k in range(G):
        out_a[k * B : (k + 1) * B, :] = p[jnp.where(first, high[k], low[k])]
        out_b[k * B : (k + 1) * B, :] = p[jnp.where(first, low[k], high[k])]


def early():
    return lax.rem(lax.axis_index("rows"), LINE) == 0


def own_part(cols, count, cmap, a, p, mh, mg, tab, t, pt, cols_s, count_s, cmap_s, sems):
    g = lax.axis_index("grp")
    copies = [
        pltpu.make_async_copy(src, dst, sems.at[n])
        for n, (src, dst) in enumerate([(cols, cols_s), (count, count_s), (cmap, cmap_s)])
    ]
    for copy in copies:
        copy.start()
    t[...] = jnp.zeros_like(t)
    mh[...] = jnp.zeros_like(mh)
    mg[...] = jnp.zeros_like(mg)
    for i in range(RB):
        pt[i] = p[i].T
    for copy in copies:
        copy.wait()
    i = jnp.int32(0)
    s = jnp.int32(0)
    for n in range(NLIVE):
        r = jnp.where(cmap_s[i] == g, 1, 0)
        t[cols_s[i, s], r] += jnp.dot(pt[i], a[i, s], preferred_element_type=F32)
        if n + 1 < NLIVE:
            over = s + 1 >= count_s[0, i]
            s = jnp.where(over, 0, s + 1)
            i = jnp.where(over, i + 1, i)

    def halves(c):
        tc = t[c].reshape(CC * B, B)
        hi = tc.astype(BF16)
        lo = (tc - hi.astype(F32)).astype(BF16)
        return jnp.concatenate([hi, lo], axis=1)

    for c in range(RB):
        add(mh, mg, CC + cmap_s[c], halves(c), p[c])
    for q in range(2 * G):
        tab[q] = halves(RB + q)


def add(mh, mg, j, lhs, tile):
    out = jnp.dot(lhs, jnp.concatenate([tile, tile], axis=0), preferred_element_type=F32)
    mh[j] += out[:B]
    mg[j] += out[B:]


def early_kernel(cols, count, cmap, a, p, pending, mh, mg, tab, passed, *scratch):
    @pl.when(early())
    def _():
        own_part(cols, count, cmap, a, p, mh, mg, tab, *scratch)


def coarse_kernel(cols, count, cmap, a, p, ghost, got_a, mh_in, mg_in, tab_in, mh, mg, tb, tab, *scratch):
    g = lax.axis_index("grp")
    h = 1 - g
    lists = ghost[...]
    js = [jnp.where(g == 0, lists[0, G + k], lists[0, k]) for k in range(G)]

    def ghosts(terms):
        for k in range(G):
            add(mh, mg, js[k], terms[G * h + k], got_a[h, k * B : (k + 1) * B, :])
        for k in range(G):
            tb[k] = terms[G * g + k]

    @pl.when(early())
    def _():
        mh[...] = mh_in[...]
        mg[...] = mg_in[...]
        ghosts(tab_in)

    @pl.when(jnp.logical_not(early()))
    def _():
        own_part(cols, count, cmap, a, p, mh, mg, tab, *scratch)
        ghosts(tab)


def known(g):
    return [4 * g, 4 * g + 1]


def message_kernel(ghost, recv, mh_in, mg_in, tb, x, rhs, mh, mg, ext, vec):
    g = lax.axis_index("grp")
    first = g == 0
    lists = ghost[...]
    js = [jnp.where(first, lists[0, k], lists[0, G + k]) for k in range(G)]
    mh[...] = mh_in[...]
    mg[...] = mg_in[...]
    outs = []
    for k in range(G):
        tile = recv[k * B : (k + 1) * B, :]
        outs.append(jnp.dot(tb[k], jnp.concatenate([tile, tile], axis=0), preferred_element_type=F32))
    for k in range(G):
        j = js[k]
        mh[j] += outs[k][:B]
        mg[j] += outs[k][B:]
    rows = recv[G * B :, :].astype(F32)
    near = rows[0:2] + rows[2:4] + rows[4:6]
    xs = [x[0:1, :], x[1:2, :], near[0:1], near[1:2]]
    js = [2, 3] + known(g)
    w_h = matvec([mh[j] for j in js], xs)
    w_g = matvec([mg[j] for j in js], xs)
    for j in range(NJ):
        hi = mh[j].astype(BF16)
        ext[j * B : (j + 1) * B, :] = hi
        ext[(NJ + j) * B : (NJ + j + 1) * B, :] = (mh[j] - hi.astype(F32)).astype(BF16)
    for q, j in enumerate(known(1 - g)):
        ext[(2 * NJ + q) * B : (2 * NJ + q + 1) * B, :] = mg[j].astype(BF16)
    rows = jnp.concatenate([w_h, rhs[...] - w_g, near], axis=0)
    ext[14 * B :, :] = padded(split3(rows))
    vec[...] = rows


def wide(exts, c, j):
    return (
        exts[c, pl.ds(pl.multiple_of(j * B, B), B), :].astype(F32)
        + exts[c, pl.ds(pl.multiple_of((NJ + j) * B, B), B), :].astype(F32)
    )


def step_kernel(exts, mh, mg, vec, x, step, base):
    g = lax.axis_index("grp")
    h = 1 - g
    first = g == 0
    rows = exts[h, 14 * B :, :].astype(F32)
    far = rows[0:4] + rows[4:8] + rows[8:12]
    xs = [far[2:3], far[3:4], vec[2:3, :], vec[3:4, :]]
    in_g = [mg[j] for j in known(h)] + [wide(exts, h, j) for j in known(g)]
    in_h = [mh[j] for j in known(h)] + [exts[h, (12 + q) * B : (13 + q) * B, :].astype(F32) for q in range(CC)]
    resid = vec[1:2, :] - far[0:1] - matvec(in_g, xs)
    resid_h = far[1:2] - vec[0:1, :] - matvec(in_h, xs)
    d_g = resid / THETA
    d_h = resid_h / THETA
    step[...] = jnp.concatenate([jnp.where(first, d_g, d_h), jnp.where(first, d_h, d_g)], axis=0)
    x_own = jnp.where(first, x[0:1, :], x[1:2, :])
    base[...] = x_own + d_g + RHO1 * RHO0 * d_g + (2.0 * RHO1 / DELTA) * resid


def sum_kernel(mg, exts, step, base_in, mats, base, op, sems):
    h = 1 - lax.axis_index("grp")
    copies = []
    for j in range(NJ):
        mats[j] = mg[j] + wide(exts, h, j)
        copies.append(pltpu.make_async_copy(mats.at[j], op.at[0, :, pl.ds(j * B, B)], sems.at[j]))
        copies[-1].start()
    own = matvec([mats[2], mats[3]], [step[0:1, :], step[1:2, :]])
    base[...] = base_in[...] - (2.0 * RHO1 / DELTA) * own
    for copy in copies:
        copy.wait()


def last_kernel(mats, ext, base, sol):
    blocks = [mats[j] for j in (0, 1, 4, 5)]
    sol[...] = base[...] - (2.0 * RHO1 / DELTA) * matvec(blocks, [ext[i : i + 1, :] for i in range(4)])


def call(kernel, out_shape, in_specs, scratch=(), out_specs=None, us=1, vm=16, **kw):
    return pl.pallas_call(
        kernel,
        out_shape=out_shape,
        in_specs=in_specs,
        out_specs=out_specs or [VMEM] * len(out_shape),
        scratch_shapes=list(scratch),
        compiler_params=pltpu.CompilerParams(vmem_limit_bytes=vm << 20),
        cost_estimate=pl.CostEstimate(flops=us * 10**9, bytes_accessed=0, transcendentals=0),
        **kw,
    )


def after_kernel(*refs):
    pass


def after(value, *others, us=AFTER_US):
    (out,) = call(
        after_kernel,
        [shaped(*value.shape, dtype=value.dtype)],
        [ANY] * (1 + len(others)),
        out_specs=[ANY],
        input_output_aliases={0: 0},
        us=us,
    )(value, *others)
    return out


def shaped(*shape, dtype=F32):
    return jax.ShapeDtypeStruct(shape, dtype)


def ints(*shape):
    return pltpu.SMEM(shape, jnp.int32)


def on_device(a_tiles, a_cols, a_count, send_lists, ghost_cols, cmap, p_tiles, x_start, coarse_rhs):
    rows = lax.axis_size("rows")
    near = []
    for c in range(rows - 1):
        near += [(2 * c + 1, 2 * c + 2), (2 * c + 2, 2 * c + 1)]

    part = shaped(NJ, B, B)
    packed = shaped(G * B + VECS, B, dtype=BF16)
    (zero,) = call(first_kernel, [shaped(8, B)], [], us=FIRST_US)()
    x = after(lax.all_gather(x_start, "grp", axis=0, tiled=True), us=SECOND_US)
    send_a, send_b, p = call(
        pack_kernel,
        [shaped(G * B, B, dtype=BF16), packed, shaped(RB, B, B, dtype=BF16)],
        [VMEM] * 4,
    )(zero, send_lists, p_tiles, x)
    terms = shaped(2 * G, CC * B, 2 * B, dtype=BF16)
    scratch = [
        pltpu.VMEM((RB + 2 * G, CC, B, B), F32),
        pltpu.VMEM((RB, B, B), BF16),
        ints(8, 15),
        ints(1, 8),
        ints(8),
        DMA((3,)),
    ]
    matrix = (a_cols, a_count, cmap, a_tiles, p)
    mh, mg, tab, send_b = call(
        early_kernel,
        [part, part, terms, packed],
        [HBM] * 3 + [VMEM] * 2 + [ANY],
        scratch,
        out_specs=[VMEM] * 3 + [ANY],
        input_output_aliases={5: 3},
        us=COARSE_US,
    )(*matrix, send_b)
    recv_b = lax.ppermute(send_b, AXES, near)
    got_a = lax.all_gather(send_a, "grp", axis=0)
    mh, mg, tb = call(
        coarse_kernel,
        [part, part, shaped(G, CC * B, 2 * B, dtype=BF16)],
        [HBM] * 3 + [VMEM] * 7,
        [pltpu.VMEM((2 * G, CC * B, 2 * B), BF16)] + scratch,
        us=COARSE_US,
    )(*matrix, ghost_cols, got_a, mh, mg, tab)
    mh, mg, ext, vec = call(
        message_kernel,
        [part, part, shaped(14 * B + VECS, B, dtype=BF16), shaped(4, B)],
        [VMEM] * 7,
    )(ghost_cols, recv_b, mh, mg, tb, x, coarse_rhs)
    exts = lax.all_gather(ext, "grp", axis=0)
    step, base = call(step_kernel, [shaped(CC, B), shaped(1, B)], [VMEM] * 5)(exts, mh, mg, vec, x)
    beyond = lax.ppermute(step, AXES, near)
    mats, base, op = call(
        sum_kernel,
        [part, shaped(1, B), shaped(1, B, NJ * B)],
        [VMEM] * 4,
        [DMA((NJ,))],
        out_specs=[VMEM, VMEM, HBM],
    )(mg, exts, step, base)
    around = lax.all_gather(after(beyond, base), "grp", axis=0, tiled=True)
    (sol,) = call(last_kernel, [shaped(1, B)], [VMEM] * 3)(mats, around, base)
    return op, sol


def solution(mesh):
    two = P(AXES, None)
    three = P(AXES, None, None)
    return jax.shard_map(
        on_device,
        mesh=mesh,
        in_specs=(P(AXES, None, None, None), two, two, two, two, P(AXES), three, two, two),
        out_specs=(three, two),
        check_vma=False,
    )
```

```python
import jax
import jax.numpy as jnp
from jax import lax
from jax.experimental import pallas as pl
from jax.experimental.pallas import tpu as pltpu
from jax.sharding import PartitionSpec as P

B = 128
RB = 8
K = 15
G = 4
CC = 2
NJ = 3 * CC
NLIVE = 40
VECS = 16
COARSE_US = 0
LINE = 12
FIRST_US = 1
SECOND_US = 1
AFTER_US = 5

THETA = 13.0
DELTA = 11.0
SIGMA = THETA / DELTA
RHO0 = 1.0 / SIGMA
RHO1 = 1.0 / (2.0 * SIGMA - RHO0)

F32 = jnp.float32
BF16 = jnp.bfloat16
AXES = ("rows", "grp")
HBM = pl.BlockSpec(memory_space=pltpu.HBM)
ANY = pl.BlockSpec(memory_space=pl.ANY)
VMEM = pl.BlockSpec(memory_space=pltpu.VMEM)
DMA = pltpu.SemaphoreType.DMA


def split3(x):
    hi = x.astype(BF16).astype(F32)
    mid = (x - hi).astype(BF16).astype(F32)
    return [hi, mid, x - hi - mid]


def padded(parts):
    rows = sum(part.shape[0] for part in parts)
    return jnp.concatenate(parts + [jnp.zeros((VECS - rows, B), F32)], axis=0).astype(BF16)


def matvec(blocks, vecs):
    acc = blocks[0] * vecs[0]
    for blk, vec in zip(blocks[1:], vecs[1:]):
        acc = acc + blk * vec
    return jnp.sum(acc.T, axis=0, keepdims=True)


def first_kernel(out):
    out[...] = jnp.zeros_like(out)


def early():
    return lax.rem(lax.axis_index("rows"), LINE) == 0


def own_part(cols, count, cmap, a, p, mh, mg, tab, t, pt, cols_s, count_s, cmap_s, sems):
    g = lax.axis_index("grp")
    copies = [
        pltpu.make_async_copy(src, dst, sems.at[n])
        for n, (src, dst) in enumerate([(cols, cols_s), (count, count_s), (cmap, cmap_s)])
    ]
    for copy in copies:
        copy.start()
    t[...] = jnp.zeros_like(t)
    mh[...] = jnp.zeros_like(mh)
    mg[...] = jnp.zeros_like(mg)
    for i in range(RB):
        pt[i] = p[i].T
    for copy in copies:
        copy.wait()
    i = jnp.int32(0)
    s = jnp.int32(0)
    for n in range(NLIVE):
        r = jnp.where(cmap_s[i] == g, 1, 0)
        t[cols_s[i, s], r] += jnp.dot(pt[i], a[i, s], preferred_element_type=F32)
        if n + 1 < NLIVE:
            over = s + 1 >= count_s[0, i]
            s = jnp.where(over, 0, s + 1)
            i = jnp.where(over, i + 1, i)

    def halves(c):
        tc = t[c].reshape(CC * B, B)
        hi = tc.astype(BF16)
        lo = (tc - hi.astype(F32)).astype(BF16)
        return jnp.concatenate([hi, lo], axis=1)

    for c in range(RB):
        add(mh, mg, CC + cmap_s[c], halves(c), p[c])
    for q in range(2 * G):
        tab[q] = halves(RB + q)


def add(mh, mg, j, lhs, tile):
    out = jnp.dot(lhs, jnp.concatenate([tile, tile], axis=0), preferred_element_type=F32)
    mh[j] += out[:B]
    mg[j] += out[B:]


def pack(zero, send, p, x, out_a, out_b, out_p):
    first = lax.axis_index("grp") == 0
    lists = send[...]
    low = [lists[0, k] for k in range(G)]
    high = [lists[0, G + k] for k in range(G)]
    out_b[G * B :, :] = padded(split3(x[...] + zero[0:1, :]))
    out_p[...] = p[...]
    for k in range(G):
        out_a[k * B : (k + 1) * B, :] = p[jnp.where(first, high[k], low[k])]
        out_b[k * B : (k + 1) * B, :] = p[jnp.where(first, low[k], high[k])]


def early_kernel(zero, send, x, cols, count, cmap, a, p, out_a, out_b, out_p, mh, mg, tab, *scratch):
    pack(zero, send, p, x, out_a, out_b, out_p)

    @pl.when(early())
    def _():
        own_part(cols, count, cmap, a, p, mh, mg, tab, *scratch)


def coarse_kernel(cols, count, cmap, a, p, ghost, got_a, mh_in, mg_in, tab_in, mh, mg, tb, tab, *scratch):
    g = lax.axis_index("grp")
    h = 1 - g
    lists = ghost[...]
    js = [jnp.where(g == 0, lists[0, G + k], lists[0, k]) for k in range(G)]

    def ghosts(terms):
        for k in range(G):
            add(mh, mg, js[k], terms[G * h + k], got_a[h, k * B : (k + 1) * B, :])
        for k in range(G):
            tb[k] = terms[G * g + k]

    @pl.when(early())
    def _():
        mh[...] = mh_in[...]
        mg[...] = mg_in[...]
        ghosts(tab_in)

    @pl.when(jnp.logical_not(early()))
    def _():
        own_part(cols, count, cmap, a, p, mh, mg, tab, *scratch)
        ghosts(tab)


def known(g):
    return [4 * g, 4 * g + 1]


def message_kernel(ghost, recv, mh_in, mg_in, tb, x, rhs, mh, mg, ext, vec):
    g = lax.axis_index("grp")
    first = g == 0
    lists = ghost[...]
    js = [jnp.where(first, lists[0, k], lists[0, G + k]) for k in range(G)]
    mh[...] = mh_in[...]
    mg[...] = mg_in[...]
    outs = []
    for k in range(G):
        tile = recv[k * B : (k + 1) * B, :]
        outs.append(jnp.dot(tb[k], jnp.concatenate([tile, tile], axis=0), preferred_element_type=F32))
    for k in range(G):
        j = js[k]
        mh[j] += outs[k][:B]
        mg[j] += outs[k][B:]
    rows = recv[G * B :, :].astype(F32)
    near = rows[0:2] + rows[2:4] + rows[4:6]
    xs = [x[0:1, :], x[1:2, :], near[0:1], near[1:2]]
    js = [2, 3] + known(g)
    w_h = matvec([mh[j] for j in js], xs)
    w_g = matvec([mg[j] for j in js], xs)
    for j in range(NJ):
        ext[j * B : (j + 1) * B, :] = mh[j].astype(BF16)
    for q, j in enumerate(known(1 - g)):
        ext[(NJ + q) * B : (NJ + q + 1) * B, :] = mg[j].astype(BF16)
    rows = jnp.concatenate([w_h, rhs[...] - w_g, near], axis=0)
    ext[8 * B :, :] = padded(split3(rows))
    vec[...] = rows


def wide(exts, c, j):
    return exts[c, pl.ds(pl.multiple_of(j * B, B), B), :].astype(F32)


def step_kernel(exts, mh, mg, vec, x, step, base):
    g = lax.axis_index("grp")
    h = 1 - g
    first = g == 0
    rows = exts[h, 8 * B :, :].astype(F32)
    far = rows[0:4] + rows[4:8] + rows[8:12]
    xs = [far[2:3], far[3:4], vec[2:3, :], vec[3:4, :]]
    in_g = [mg[j] for j in known(h)] + [wide(exts, h, j) for j in known(g)]
    in_h = [mh[j] for j in known(h)] + [exts[h, (NJ + q) * B : (NJ + q + 1) * B, :].astype(F32) for q in range(CC)]
    resid = vec[1:2, :] - far[0:1] - matvec(in_g, xs)
    resid_h = far[1:2] - vec[0:1, :] - matvec(in_h, xs)
    d_g = resid / THETA
    d_h = resid_h / THETA
    step[...] = jnp.concatenate([jnp.where(first, d_g, d_h), jnp.where(first, d_h, d_g)], axis=0)
    x_own = jnp.where(first, x[0:1, :], x[1:2, :])
    base[...] = x_own + d_g + RHO1 * RHO0 * d_g + (2.0 * RHO1 / DELTA) * resid


def sum_kernel(mg, exts, step, base_in, mats, base, op, sems):
    h = 1 - lax.axis_index("grp")
    copies = []
    for j in range(NJ):
        mats[j] = mg[j] + wide(exts, h, j)
        copies.append(pltpu.make_async_copy(mats.at[j], op.at[0, :, pl.ds(j * B, B)], sems.at[j]))
        copies[-1].start()
    own = matvec([mats[2], mats[3]], [step[0:1, :], step[1:2, :]])
    base[...] = base_in[...] - (2.0 * RHO1 / DELTA) * own
    for copy in copies:
        copy.wait()


def last_kernel(mats, ext, base, sol):
    blocks = [mats[j] for j in (0, 1, 4, 5)]
    sol[...] = base[...] - (2.0 * RHO1 / DELTA) * matvec(blocks, [ext[i : i + 1, :] for i in range(4)])


def call(kernel, out_shape, in_specs, scratch=(), out_specs=None, us=1, vm=16, **kw):
    return pl.pallas_call(
        kernel,
        out_shape=out_shape,
        in_specs=in_specs,
        out_specs=out_specs or [VMEM] * len(out_shape),
        scratch_shapes=list(scratch),
        compiler_params=pltpu.CompilerParams(vmem_limit_bytes=vm << 20),
        cost_estimate=pl.CostEstimate(flops=us * 10**9, bytes_accessed=0, transcendentals=0),
        **kw,
    )


def after_kernel(*refs):
    pass


def after(value, *others, us=AFTER_US):
    (out,) = call(
        after_kernel,
        [shaped(*value.shape, dtype=value.dtype)],
        [ANY] * (1 + len(others)),
        out_specs=[ANY],
        input_output_aliases={0: 0},
        us=us,
    )(value, *others)
    return out


def shaped(*shape, dtype=F32):
    return jax.ShapeDtypeStruct(shape, dtype)


def ints(*shape):
    return pltpu.SMEM(shape, jnp.int32)


def on_device(a_tiles, a_cols, a_count, send_lists, ghost_cols, cmap, p_tiles, x_start, coarse_rhs):
    rows = lax.axis_size("rows")
    near = []
    for c in range(rows - 1):
        near += [(2 * c + 1, 2 * c + 2), (2 * c + 2, 2 * c + 1)]

    part = shaped(NJ, B, B)
    packed = shaped(G * B + VECS, B, dtype=BF16)
    (zero,) = call(first_kernel, [shaped(8, B)], [], us=FIRST_US)()
    x = after(lax.all_gather(x_start, "grp", axis=0, tiled=True), us=SECOND_US)
    terms = shaped(2 * G, CC * B, 2 * B, dtype=BF16)
    scratch = [
        pltpu.VMEM((RB + 2 * G, CC, B, B), F32),
        pltpu.VMEM((RB, B, B), BF16),
        ints(8, 15),
        ints(1, 8),
        ints(8),
        DMA((3,)),
    ]
    matrix = (a_cols, a_count, cmap, a_tiles)
    send_a, send_b, p, mh, mg, tab = call(
        early_kernel,
        [shaped(G * B, B, dtype=BF16), packed, shaped(RB, B, B, dtype=BF16), part, part, terms],
        [VMEM] * 3 + [HBM] * 3 + [VMEM] * 2,
        scratch,
        us=COARSE_US,
    )(zero, send_lists, x, *matrix, p_tiles)
    recv_b = lax.ppermute(send_b, AXES, near)
    got_a = lax.all_gather(send_a, "grp", axis=0)
    mh, mg, tb = call(
        coarse_kernel,
        [part, part, shaped(G, CC * B, 2 * B, dtype=BF16)],
        [HBM] * 3 + [VMEM] * 7,
        [pltpu.VMEM((2 * G, CC * B, 2 * B), BF16)] + scratch,
        us=COARSE_US,
    )(*matrix, p, ghost_cols, got_a, mh, mg, tab)
    mh, mg, ext, vec = call(
        message_kernel,
        [part, part, shaped(8 * B + VECS, B, dtype=BF16), shaped(4, B)],
        [VMEM] * 7,
    )(ghost_cols, recv_b, mh, mg, tb, x, coarse_rhs)
    exts = lax.all_gather(ext, "grp", axis=0)
    step, base = call(step_kernel, [shaped(CC, B), shaped(1, B)], [VMEM] * 5)(exts, mh, mg, vec, x)
    beyond = lax.ppermute(step, AXES, near)
    mats, base, op = call(
        sum_kernel,
        [part, shaped(1, B), shaped(1, B, NJ * B)],
        [VMEM] * 4,
        [DMA((NJ,))],
        out_specs=[VMEM, VMEM, HBM],
    )(mg, exts, step, base)
    around = lax.all_gather(after(beyond, base), "grp", axis=0, tiled=True)
    (sol,) = call(last_kernel, [shaped(1, B)], [VMEM] * 3)(mats, around, base)
    return op, sol


def solution(mesh):
    two = P(AXES, None)
    three = P(AXES, None, None)
    return jax.shard_map(
        on_device,
        mesh=mesh,
        in_specs=(P(AXES, None, None, None), two, two, two, two, P(AXES), three, two, two),
        out_specs=(three, two),
        check_vma=False,
    )
```

```python
import jax
import jax.numpy as jnp
from jax import lax
from jax.experimental import pallas as pl
from jax.experimental.pallas import tpu as pltpu
from jax.sharding import PartitionSpec as P

B = 128
RB = 8
K = 15
G = 4
CC = 2
NJ = 3 * CC
NLIVE = 40
VECS = 16
COARSE_US = 0
LINE = 12
FIRST_US = 1
SECOND_US = 1
AFTER_US = 5

THETA = 13.0
DELTA = 11.0
SIGMA = THETA / DELTA
RHO0 = 1.0 / SIGMA
RHO1 = 1.0 / (2.0 * SIGMA - RHO0)

F32 = jnp.float32
BF16 = jnp.bfloat16
AXES = ("rows", "grp")
HBM = pl.BlockSpec(memory_space=pltpu.HBM)
ANY = pl.BlockSpec(memory_space=pl.ANY)
VMEM = pl.BlockSpec(memory_space=pltpu.VMEM)
DMA = pltpu.SemaphoreType.DMA


def split3(x):
    hi = x.astype(BF16).astype(F32)
    mid = (x - hi).astype(BF16).astype(F32)
    return [hi, mid, x - hi - mid]


def padded(parts):
    rows = sum(part.shape[0] for part in parts)
    return jnp.concatenate(parts + [jnp.zeros((VECS - rows, B), F32)], axis=0).astype(BF16)


def matvec(blocks, vecs):
    acc = blocks[0] * vecs[0]
    for blk, vec in zip(blocks[1:], vecs[1:]):
        acc = acc + blk * vec
    return jnp.sum(acc.T, axis=0, keepdims=True)


def first_kernel(out):
    out[...] = jnp.zeros_like(out)


def early():
    return lax.rem(lax.axis_index("rows"), LINE) == 0


def own_part(cols, count, cmap, a, p, mh, mg, tab, t, pt, cols_s, count_s, cmap_s, sems):
    g = lax.axis_index("grp")
    copies = [
        pltpu.make_async_copy(src, dst, sems.at[n])
        for n, (src, dst) in enumerate([(cols, cols_s), (count, count_s), (cmap, cmap_s)])
    ]
    for copy in copies:
        copy.start()
    t[...] = jnp.zeros_like(t)
    mh[...] = jnp.zeros_like(mh)
    mg[...] = jnp.zeros_like(mg)
    for i in range(RB):
        pt[i] = p[i].T
    for copy in copies:
        copy.wait()
    i = jnp.int32(0)
    s = jnp.int32(0)
    for n in range(NLIVE):
        r = jnp.where(cmap_s[i] == g, 1, 0)
        t[cols_s[i, s], r] += jnp.dot(pt[i], a[i, s], preferred_element_type=F32)
        if n + 1 < NLIVE:
            over = s + 1 >= count_s[0, i]
            s = jnp.where(over, 0, s + 1)
            i = jnp.where(over, i + 1, i)

    def halves(c):
        tc = t[c].reshape(CC * B, B)
        hi = tc.astype(BF16)
        lo = (tc - hi.astype(F32)).astype(BF16)
        return jnp.concatenate([hi, lo], axis=1)

    for c in range(RB):
        add(mh, mg, CC + cmap_s[c], halves(c), p[c])
    for q in range(2 * G):
        tab[q] = halves(RB + q)


def add(mh, mg, j, lhs, tile):
    out = jnp.dot(lhs, jnp.concatenate([tile, tile], axis=0), preferred_element_type=F32)
    mh[j] += out[:B]
    mg[j] += out[B:]


def pack(zero, send, p, x, out_a, out_b, out_p):
    first = lax.axis_index("grp") == 0
    lists = send[...]
    low = [lists[0, k] for k in range(G)]
    high = [lists[0, G + k] for k in range(G)]
    out_b[G * B :, :] = padded(split3(x[...] + zero[0:1, :]))
    out_p[...] = p[...]
    for k in range(G):
        out_a[k * B : (k + 1) * B, :] = p[jnp.where(first, high[k], low[k])]
        out_b[k * B : (k + 1) * B, :] = p[jnp.where(first, low[k], high[k])]


def early_kernel(zero, send, x, cols, count, cmap, a, p, out_a, out_b, out_p, mh, mg, tab, *scratch):
    pack(zero, send, p, x, out_a, out_b, out_p)

    @pl.when(early())
    def _():
        own_part(cols, count, cmap, a, p, mh, mg, tab, *scratch)


def coarse_kernel(cols, count, cmap, a, p, ghost, got_a, mh_in, mg_in, tab_in, mh, mg, tb, tab, *scratch):
    g = lax.axis_index("grp")
    h = 1 - g
    lists = ghost[...]
    js = [jnp.where(g == 0, lists[0, G + k], lists[0, k]) for k in range(G)]

    def ghosts(terms):
        for k in range(G):
            add(mh, mg, js[k], terms[G * h + k], got_a[h, k * B : (k + 1) * B, :])
        for k in range(G):
            tb[k] = terms[G * g + k]

    @pl.when(early())
    def _():
        mh[...] = mh_in[...]
        mg[...] = mg_in[...]
        ghosts(tab_in)

    @pl.when(jnp.logical_not(early()))
    def _():
        own_part(cols, count, cmap, a, p, mh, mg, tab, *scratch)
        ghosts(tab)


def known(g):
    return [4 * g, 4 * g + 1]


def message_kernel(ghost, recv, mh_in, mg_in, tb, x, rhs, mh, mg, ext, vec, table):
    g = lax.axis_index("grp")
    first = g == 0
    lists = ghost[...]
    js = [jnp.where(first, lists[0, k], lists[0, G + k]) for k in range(G)]
    rows = recv[G * B :, :].astype(F32)
    near = rows[0:2] + rows[2:4] + rows[4:6]
    none = jnp.zeros_like(near)
    table[...] = jnp.concatenate([jnp.where(first, near, none), x[...], jnp.where(first, none, near), none], axis=0)
    outs = []
    for k in range(G):
        tile = recv[k * B : (k + 1) * B, :]
        outs.append(jnp.dot(tb[k], jnp.concatenate([tile, tile], axis=0), preferred_element_type=F32))
    xs = [x[0:1, :], x[1:2, :], near[0:1], near[1:2]] + [table[pl.ds(js[k], 1), :] for k in range(G)]
    at = [2, 3] + known(g)
    w_h = matvec([mh_in[j] for j in at] + [out[:B] for out in outs], xs)
    w_g = matvec([mg_in[j] for j in at] + [out[B:] for out in outs], xs)
    mh[...] = mh_in[...]
    mg[...] = mg_in[...]
    for k in range(G):
        mh[js[k]] += outs[k][:B]
        mg[js[k]] += outs[k][B:]
    for j in range(NJ):
        ext[j * B : (j + 1) * B, :] = mh[j].astype(BF16)
    for q, j in enumerate(known(1 - g)):
        ext[(NJ + q) * B : (NJ + q + 1) * B, :] = mg[j].astype(BF16)
    rows = jnp.concatenate([w_h, rhs[...] - w_g, near], axis=0)
    ext[8 * B :, :] = padded(split3(rows))
    vec[...] = rows


def wide(exts, c, j):
    return exts[c, pl.ds(pl.multiple_of(j * B, B), B), :].astype(F32)


def step_kernel(exts, mh, mg, vec, x, step, base):
    g = lax.axis_index("grp")
    h = 1 - g
    first = g == 0
    rows = exts[h, 8 * B :, :].astype(F32)
    far = rows[0:4] + rows[4:8] + rows[8:12]
    xs = [far[2:3], far[3:4], vec[2:3, :], vec[3:4, :]]
    in_g = [mg[j] for j in known(h)] + [wide(exts, h, j) for j in known(g)]
    in_h = [mh[j] for j in known(h)] + [exts[h, (NJ + q) * B : (NJ + q + 1) * B, :].astype(F32) for q in range(CC)]
    resid = vec[1:2, :] - far[0:1] - matvec(in_g, xs)
    resid_h = far[1:2] - vec[0:1, :] - matvec(in_h, xs)
    d_g = resid / THETA
    d_h = resid_h / THETA
    step[...] = jnp.concatenate([jnp.where(first, d_g, d_h), jnp.where(first, d_h, d_g)], axis=0)
    x_own = jnp.where(first, x[0:1, :], x[1:2, :])
    base[...] = x_own + d_g + RHO1 * RHO0 * d_g + (2.0 * RHO1 / DELTA) * resid


def sum_kernel(mg, exts, step, base_in, mats, base, op, sems):
    h = 1 - lax.axis_index("grp")
    copies = []
    for j in range(NJ):
        mats[j] = mg[j] + wide(exts, h, j)
        copies.append(pltpu.make_async_copy(mats.at[j], op.at[0, :, pl.ds(j * B, B)], sems.at[j]))
        copies[-1].start()
    own = matvec([mats[2], mats[3]], [step[0:1, :], step[1:2, :]])
    base[...] = base_in[...] - (2.0 * RHO1 / DELTA) * own
    for copy in copies:
        copy.wait()


def last_kernel(mats, ext, base, sol):
    blocks = [mats[j] for j in (0, 1, 4, 5)]
    sol[...] = base[...] - (2.0 * RHO1 / DELTA) * matvec(blocks, [ext[i : i + 1, :] for i in range(4)])


def call(kernel, out_shape, in_specs, scratch=(), out_specs=None, us=1, vm=16, **kw):
    return pl.pallas_call(
        kernel,
        out_shape=out_shape,
        in_specs=in_specs,
        out_specs=out_specs or [VMEM] * len(out_shape),
        scratch_shapes=list(scratch),
        compiler_params=pltpu.CompilerParams(vmem_limit_bytes=vm << 20),
        cost_estimate=pl.CostEstimate(flops=us * 10**9, bytes_accessed=0, transcendentals=0),
        **kw,
    )


def after_kernel(*refs):
    pass


def after(value, *others, us=AFTER_US):
    (out,) = call(
        after_kernel,
        [shaped(*value.shape, dtype=value.dtype)],
        [ANY] * (1 + len(others)),
        out_specs=[ANY],
        input_output_aliases={0: 0},
        us=us,
    )(value, *others)
    return out


def shaped(*shape, dtype=F32):
    return jax.ShapeDtypeStruct(shape, dtype)


def ints(*shape):
    return pltpu.SMEM(shape, jnp.int32)


def on_device(a_tiles, a_cols, a_count, send_lists, ghost_cols, cmap, p_tiles, x_start, coarse_rhs):
    rows = lax.axis_size("rows")
    near = []
    for c in range(rows - 1):
        near += [(2 * c + 1, 2 * c + 2), (2 * c + 2, 2 * c + 1)]

    part = shaped(NJ, B, B)
    packed = shaped(G * B + VECS, B, dtype=BF16)
    (zero,) = call(first_kernel, [shaped(8, B)], [], us=FIRST_US)()
    x = after(lax.all_gather(x_start, "grp", axis=0, tiled=True), us=SECOND_US)
    terms = shaped(2 * G, CC * B, 2 * B, dtype=BF16)
    scratch = [
        pltpu.VMEM((RB + 2 * G, CC, B, B), F32),
        pltpu.VMEM((RB, B, B), BF16),
        ints(8, 15),
        ints(1, 8),
        ints(8),
        DMA((3,)),
    ]
    matrix = (a_cols, a_count, cmap, a_tiles)
    send_a, send_b, p, mh, mg, tab = call(
        early_kernel,
        [shaped(G * B, B, dtype=BF16), packed, shaped(RB, B, B, dtype=BF16), part, part, terms],
        [VMEM] * 3 + [HBM] * 3 + [VMEM] * 2,
        scratch,
        us=COARSE_US,
    )(zero, send_lists, x, *matrix, p_tiles)
    recv_b = lax.ppermute(send_b, AXES, near)
    got_a = lax.all_gather(send_a, "grp", axis=0)
    mh, mg, tb = call(
        coarse_kernel,
        [part, part, shaped(G, CC * B, 2 * B, dtype=BF16)],
        [HBM] * 3 + [VMEM] * 7,
        [pltpu.VMEM((2 * G, CC * B, 2 * B), BF16)] + scratch,
        us=COARSE_US,
    )(*matrix, p, ghost_cols, got_a, mh, mg, tab)
    mh, mg, ext, vec = call(
        message_kernel,
        [part, part, shaped(8 * B + VECS, B, dtype=BF16), shaped(4, B)],
        [VMEM] * 7,
        [pltpu.VMEM((8, B), F32)],
    )(ghost_cols, recv_b, mh, mg, tb, x, coarse_rhs)
    exts = lax.all_gather(ext, "grp", axis=0)
    step, base = call(step_kernel, [shaped(CC, B), shaped(1, B)], [VMEM] * 5)(exts, mh, mg, vec, x)
    beyond = lax.ppermute(step, AXES, near)
    mats, base, op = call(
        sum_kernel,
        [part, shaped(1, B), shaped(1, B, NJ * B)],
        [VMEM] * 4,
        [DMA((NJ,))],
        out_specs=[VMEM, VMEM, HBM],
    )(mg, exts, step, base)
    around = lax.all_gather(after(beyond, base), "grp", axis=0, tiled=True)
    (sol,) = call(last_kernel, [shaped(1, B)], [VMEM] * 3)(mats, around, base)
    return op, sol


def solution(mesh):
    two = P(AXES, None)
    three = P(AXES, None, None)
    return jax.shard_map(
        on_device,
        mesh=mesh,
        in_specs=(P(AXES, None, None, None), two, two, two, two, P(AXES), three, two, two),
        out_specs=(three, two),
        check_vma=False,
    )
```
